32 devices in a mesh: dp: 8 (over y, x, core), expert: 4 (over z).
Axes of the slice: x: 2, y: 2, z: 4, core: 2. Of those that a mesh axis runs over, the one named last changes fastest.
Arguments:
- tokens: bfloat16 [1024, 3584], P('dp', 'expert'), may hold values from -6 to 6
- gate_weight: bfloat16 [4, 1536, 3584], P('expert', 'dp'), may hold values from -0.09375 to 0.09375
- up_weight: bfloat16 [4, 1536, 3584], P('expert', 'dp'), may hold values from -0.09375 to 0.09375
- down_weight: bfloat16 [4, 1536, 3584], P('expert', 'dp'), may hold values from -0.15625 to 0.15625
- slot_tokens: int32 [4, 8], P(None, 'dp'), may hold values from 0 to 127
- slot_weights: float32 [4, 8], P(None, 'dp'), may hold values from 0.2 to 1
- out_grad: bfloat16 [1024, 3584], P('dp', 'expert'), may hold values from -6 to 6
Outputs:
- token_grad: bfloat16 [1024, 3584], P('dp', 'expert')
- gate_grad: bfloat16 [4, 1536, 3584], P('expert', 'dp')
- up_grad: bfloat16 [4, 1536, 3584], P('expert', 'dp')
- down_grad: bfloat16 [4, 1536, 3584], P('expert', 'dp')
The draws below stay inside these ranges and needn't reach their ends.
Inputs may be any that keep to these rules, and one draw needn't show every extreme that they name: `slot_tokens`: slot c of an expert names a token of data index c // 1 by its row among that index's 128 tokens.
All inputs are finite; a program needn't handle non-finite values.
Results may differ from the reference program's by a relative error of at most 0.0057.
Values may be sent and summed in bfloat16 or wider, within the bound.
A program may use at most 64 MiB of HBM per device.

```python
import math
import jax
import jax.numpy as jnp

D = 3584
FF = 1536
CAP_ROW = 1
TOK_ROW = 128
EXPERTS = 4
CAP = 8
TOKENS = 1024


def place_ends(drawn, key, smallest, high):
    longest = drawn.shape.index(max(drawn.shape))
    spots = []
    for shift in (0, 1):
        where = [jax.random.randint(jax.random.fold_in(key, axis), (), 0, length) for axis, length in enumerate(drawn.shape)]
        where[longest] = (where[longest] + shift) % drawn.shape[longest]
        spots.append(tuple(where))
    return drawn.at[spots[0]].set(smallest).at[spots[1]].set(high)


def levels(rng, shape, cuts, smallest, largest):
    gain, own = 1.0, jax.random.fold_in(rng, 6)
    for axis_at, shards_of in cuts:
        draws = jnp.exp(jax.random.uniform(jax.random.fold_in(own, axis_at), (shards_of,), jnp.float32, smallest / len(cuts), largest / len(cuts)))
        gain = gain * jnp.repeat(draws, shape[axis_at] // shards_of).reshape([-1 if axis == axis_at else 1 for axis in range(len(shape))])
    return gain


def normal_values(own_key, shape, deviation, limit, split=(), held_as=jnp.bfloat16):
    gain = levels(own_key, shape, split, -0.22, 0.18) if split else 1.0
    drawn = jax.random.normal(own_key, shape, jnp.float32) * deviation * gain
    return jnp.minimum(jnp.maximum(drawn, -limit), limit).astype(held_as)


def setup_inputs(seed: int = 0) -> dict:
    key_of = jax.random.split(jax.random.key(seed), 8)
    return {
        "tokens": normal_values(key_of[0], (TOKENS, D), 1.0, 6.0, ((0, 8), (1, 4))),
        "gate_weight": normal_values(key_of[1], (EXPERTS, FF, D), D ** -0.5, 0.09375, ((0, 4), (1, 8))),
        "up_weight": normal_values(key_of[2], (EXPERTS, FF, D), D ** -0.5, 0.09375, ((0, 4), (1, 8))),
        "down_weight": normal_values(key_of[3], (EXPERTS, FF, D), FF ** -0.5, 0.15625, ((0, 4), (1, 8))),
        "slot_tokens": place_ends(jax.random.randint(key_of[4], (EXPERTS, CAP), 0, TOK_ROW), jax.random.fold_in(key_of[4], 1), 0, TOK_ROW - 1).astype(jnp.int32),
        "slot_weights": jnp.clip(jnp.exp(math.log(1.0) - 1.609438 * jax.random.uniform(key_of[5], (EXPERTS, CAP), jnp.float32) ** levels(key_of[5], (EXPERTS, CAP), ((1, 8),), -0.2, 0.2)), 0.2, 1.0),
        "out_grad": normal_values(key_of[6], (TOKENS, D), 1.0, 6.0, ((0, 8), (1, 4))),
    }


def reference(tokens, gate_weight, up_weight, down_weight, slot_tokens, slot_weights, out_grad):
    base_rows = ((jnp.arange(CAP) // CAP_ROW) * TOK_ROW).astype(jnp.int32)
    rows = (base_rows[None, :] + slot_tokens).astype(jnp.int32)
    flat_rows = rows.reshape(-1)
    picked = tokens[rows]
    picked32 = picked.astype(jnp.float32)
    gate32 = gate_weight.astype(jnp.float32)
    up32 = up_weight.astype(jnp.float32)
    down32 = down_weight.astype(jnp.float32)
    gate_pre = jnp.einsum('ecd,efd->ecf', picked32, gate32)
    up_pre = jnp.einsum('ecd,efd->ecf', picked32, up32)
    sigmoid_gate = jax.nn.sigmoid(gate_pre)
    activated = gate_pre * sigmoid_gate
    hidden = (activated * up_pre).astype(jnp.bfloat16)
    slot_grad = (slot_weights[:, :, None] * out_grad[rows].astype(jnp.float32)).astype(jnp.bfloat16)
    slot_grad32 = slot_grad.astype(jnp.float32)
    hidden_grad = jnp.einsum('ecd,efd->ecf', slot_grad32, down32)
    gate_back = (hidden_grad * up_pre * sigmoid_gate * (1.0 + gate_pre * (1.0 - sigmoid_gate))).astype(jnp.bfloat16)
    up_back = (hidden_grad * activated).astype(jnp.bfloat16)
    gate_back32 = gate_back.astype(jnp.float32)
    up_back32 = up_back.astype(jnp.float32)
    down_grad = jnp.einsum('ecf,ecd->efd', hidden.astype(jnp.float32), slot_grad32).astype(jnp.bfloat16)
    gate_grad = jnp.einsum('ecf,ecd->efd', gate_back32, picked32).astype(jnp.bfloat16)
    up_grad = jnp.einsum('ecf,ecd->efd', up_back32, picked32).astype(jnp.bfloat16)
    slot_input_grad = jnp.einsum('ecf,efd->ecd', gate_back32, gate32) + jnp.einsum('ecf,efd->ecd', up_back32, up32)
    scaled_grad = (slot_weights[:, :, None] * slot_input_grad).reshape(-1, D)
    token_grad = out_grad.astype(jnp.float32).at[flat_rows].add(scaled_grad).astype(jnp.bfloat16)
    return token_grad, gate_grad, up_grad, down_grad
```

```python
import functools

import jax
import jax.numpy as jnp
from jax import lax
from jax.experimental import pallas as pl
from jax.experimental.pallas import tpu as pltpu
from jax.sharding import PartitionSpec as P

MESH = pl.DeviceIdType.MESH
LANES = 128
F32 = jnp.float32
BF16 = jnp.bfloat16


def up_to(value, unit):
    return -(-value // unit) * unit


def each(count, body):
    if count <= 16:
        for i in range(count):
            body(i)
    else:
        lax.fori_loop(0, count, lambda i, carry: (body(i), carry)[1], 0)


def across(a, b):
    return lax.dot_general(a, b, (((1,), (1,)), ((), ())), preferred_element_type=F32)


def exchange_kernel(
    rows, experts, tokens, grads, gate_w, up_w, down_w, slots, weights,
    inputs_out, cotangents_out, backs_out, returned,
    tokens_v, grads_v, weights_v, stage, held, spread, sums, parts, total,
    load_sem, weight_sem, s1, r1, s2, r2, s3, r3, s4, r4,
):
    row, col = lax.axis_index("dp"), lax.axis_index("expert")
    width = tokens.shape[1]
    pieces = width // LANES
    pad16 = stage.shape[1]
    pad8 = returned.shape[1]

    loads = [
        pltpu.make_async_copy(tokens, tokens_v, load_sem.at[0]),
        pltpu.make_async_copy(grads, grads_v, load_sem.at[1]),
    ]
    weight_loads = [
        pltpu.make_async_copy(ref.at[0], weights_v.at[i], weight_sem.at[i])
        for i, ref in enumerate((gate_w, up_w, down_w))
    ]
    for load in loads:
        load.start()

    def other_row(i):
        return lax.rem(row + i + 1, rows)

    def other_col(i):
        return lax.rem(col + i + 1, experts)

    barrier = pltpu.get_barrier_semaphore()
    each(experts - 1, lambda i: pl.semaphore_signal(
        barrier, inc=1, device_id=(row, other_col(i)), device_id_type=MESH))
    each(rows - 1, lambda i: pl.semaphore_signal(
        barrier, inc=1, device_id=(other_row(i), col), device_id_type=MESH))
    for load in weight_loads:
        load.start()

    hot = (
        lax.broadcasted_iota(jnp.int32, (experts, tokens.shape[0]), 1) == slots[...]
    ).astype(F32).astype(BF16)
    loads[0].wait()
    picked = jnp.dot(hot, tokens_v[...], preferred_element_type=F32)
    loads[1].wait()
    scaled = weights[...] * jnp.dot(hot, grads_v[...], preferred_element_type=F32)
    block = [picked[:, j * LANES:(j + 1) * LANES][:, None] for j in range(pieces)]
    block += [scaled[:, j * LANES:(j + 1) * LANES][:, None] for j in range(pieces)]
    if pad16 > 2 * pieces:
        block.append(jnp.zeros((experts, pad16 - 2 * pieces, LANES), F32))
    stage[...] = jnp.concatenate(block, axis=1).astype(BF16)
    mine = pl.ds(pl.multiple_of(col * pad16, pad16), pad16)
    held[row, mine] = stage[col]
    pl.semaphore_wait(barrier, rows + experts - 2)

    def first(to, source):
        at = pl.ds(pl.multiple_of(source * pad16, pad16), pad16)
        return pltpu.make_async_remote_copy(
            src_ref=stage.at[to], dst_ref=held.at[row, at],
            send_sem=s1.at[to], recv_sem=r1.at[source],
            device_id=(row, to), device_id_type=MESH)

    each(experts - 1, lambda i: first(other_col(i), col).start())
    each(experts - 1, lambda i: first(col, other_col(i)).wait_recv())

    def second(to, source):
        return pltpu.make_async_remote_copy(
            src_ref=held.at[source], dst_ref=held.at[source],
            send_sem=s2.at[to], recv_sem=r2.at[source],
            device_id=(to, col), device_id_type=MESH)

    each(rows - 1, lambda i: second(other_row(i), row).start())

    def widen(source):
        size = experts * pad16
        spread[pl.ds(pl.multiple_of(source * size, size), size)] = held[source].astype(F32)

    widen(row)

    def arrive(i):
        source = other_row(i)
        second(row, source).wait_recv()
        widen(source)

    each(rows - 1, arrive)

    def whole_rows(base):
        return jnp.concatenate([
            spread[pl.ds(z * pad16 + base + j, rows, stride=experts * pad16), :]
            for z in range(experts) for j in range(pieces)
        ], axis=1).astype(BF16)

    inputs = whole_rows(0)
    cotangents = whole_rows(pieces)
    inputs_out[...] = inputs
    cotangents_out[...] = cotangents

    weight_loads[0].wait()
    gate_pre = across(inputs, weights_v[0])
    weight_loads[1].wait()
    up_pre = across(inputs, weights_v[1])
    weight_loads[2].wait()
    hidden_grad = across(cotangents, weights_v[2])
    sigmoid = jax.nn.sigmoid(gate_pre)
    activated = gate_pre * sigmoid
    hidden = (activated * up_pre).astype(BF16)
    gate_back = (
        hidden_grad * up_pre * sigmoid * (1.0 + gate_pre * (1.0 - sigmoid))
    ).astype(BF16)
    up_back = (hidden_grad * activated).astype(BF16)
    part = jnp.dot(gate_back, weights_v[0], preferred_element_type=F32)
    part += jnp.dot(up_back, weights_v[1], preferred_element_type=F32)
    for z in range(experts):
        for j in range(pieces):
            at = (z * pieces + j) * LANES
            parts[pl.ds(z * pad8 + j, rows, stride=experts * pad8), :] = part[:, at:at + LANES]
    slab = experts * pad8

    def third(to, source):
        return pltpu.make_async_remote_copy(
            src_ref=parts.at[pl.ds(pl.multiple_of(to * slab, slab), slab)],
            dst_ref=sums.at[source],
            send_sem=s3.at[to], recv_sem=r3.at[source],
            device_id=(to, col), device_id_type=MESH)

    each(rows - 1, lambda i: third(other_row(i), row).start())
    for i, value in enumerate((gate_back, up_back, hidden)):
        backs_out[i] = value
    total[...] = parts[pl.ds(pl.multiple_of(row * slab, slab), slab)]

    def gather_sum(i):
        source = other_row(i)
        third(row, source).wait_recv()
        total[...] += sums[source]

    each(rows - 1, gather_sum)

    def fourth(to, source):
        return pltpu.make_async_remote_copy(
            src_ref=total.at[pl.ds(pl.multiple_of(to * pad8, pad8), pad8)],
            dst_ref=returned.at[source],
            send_sem=s4.at[to], recv_sem=r4.at[source],
            device_id=(row, to), device_id_type=MESH)

    each(experts - 1, lambda i: fourth(other_col(i), col).start())
    returned[col] = total[pl.ds(pl.multiple_of(col * pad8, pad8), pad8)]

    each(experts - 1, lambda i: first(other_col(i), col).wait_send())
    each(rows - 1, lambda i: second(other_row(i), row).wait_send())
    each(rows - 1, lambda i: third(other_row(i), row).wait_send())
    each(experts - 1, lambda i: fourth(col, other_col(i)).wait_recv())
    each(experts - 1, lambda i: fourth(other_col(i), col).wait_send())


def exchange(mesh, tokens, gate_w, up_w, down_w, slots, weights, grads):
    rows, experts = mesh.shape["dp"], mesh.shape["expert"]
    width = tokens.shape[1]
    units, features = gate_w.shape[1:]
    pieces = width // LANES
    pad16, pad8 = up_to(2 * pieces, 16), up_to(pieces, 8)
    dma = pltpu.SemaphoreType.DMA
    hbm = pl.BlockSpec(memory_space=pl.ANY)
    vmem = pl.BlockSpec(memory_space=pltpu.VMEM)
    return pl.pallas_call(
        functools.partial(exchange_kernel, rows, experts),
        out_shape=(
            jax.ShapeDtypeStruct((rows, features), BF16),
            jax.ShapeDtypeStruct((rows, features), BF16),
            jax.ShapeDtypeStruct((3, rows, units), BF16),
            jax.ShapeDtypeStruct((experts, pad8, LANES), F32),
        ),
        in_specs=[hbm] * 5 + [vmem] * 2,
        out_specs=(vmem,) * 4,
        scratch_shapes=[
            pltpu.VMEM(tokens.shape, BF16),
            pltpu.VMEM(grads.shape, BF16),
            pltpu.VMEM((3, units, features), BF16),
            pltpu.VMEM((experts, pad16, LANES), BF16),
            pltpu.VMEM((rows, experts * pad16, LANES), BF16),
            pltpu.VMEM((rows * experts * pad16, LANES), F32),
            pltpu.VMEM((rows, experts * pad8, LANES), F32),
            pltpu.VMEM((rows * experts * pad8, LANES), F32),
            pltpu.VMEM((experts * pad8, LANES), F32),
            dma((2,)), dma((3,)),
            dma((experts,)), dma((experts,)), dma((rows,)), dma((rows,)),
            dma((rows,)), dma((rows,)), dma((experts,)), dma((experts,)),
        ],
        compiler_params=pltpu.CompilerParams(
            collective_id=0, has_side_effects=True, vmem_limit_bytes=44 << 20),
        name="exchange",
    )(tokens, grads, gate_w, up_w, down_w, slots, weights)


def finish_kernel(
    inputs, cotangents, backs, returned, grads, slots, weights,
    token_out, gate_out, up_out, down_out,
    wide, token_v, sems, token_sem,
):
    count, units, features = wide.shape
    experts = returned.shape[0]
    width = token_v.shape[1]
    chunk = 64 if units % 64 == 0 else units
    copies = []
    for i, out in enumerate((gate_out, up_out, down_out)):
        back = backs[i].astype(F32).T.astype(BF16)
        other = cotangents if i == 2 else inputs
        for k in range(units // chunk):
            at = pl.ds(k * chunk, chunk)
            wide[i, at] = jnp.dot(
                back[k * chunk:(k + 1) * chunk], other[...], preferred_element_type=F32
            ).astype(BF16)
            copy = pltpu.make_async_copy(
                wide.at[i, at], out.at[0, at], sems.at[i * (units // chunk) + k])
            copy.start()
            copies.append(copy)
    place = lax.broadcasted_iota(jnp.int32, (token_v.shape[0], LANES), 0)
    masks = [place == slots[e, 0] for e in range(experts)]
    for j in range(width // LANES):
        at = pl.ds(j * LANES, LANES)
        value = grads[:, at].astype(F32)
        for e in range(experts):
            line = weights[e, 0] * returned[e, pl.ds(j, 1), :]
            value += jnp.where(masks[e], line, 0.0)
        token_v[:, at] = value.astype(BF16)
    copy = pltpu.make_async_copy(token_v, token_out, token_sem)
    copy.start()
    copies.append(copy)
    for copy in copies:
        copy.wait()


def finish(inputs, cotangents, backs, returned, grads, slots, weights, like):
    units, features = like.shape[1:]
    hbm = pl.BlockSpec(memory_space=pl.ANY)
    vmem = pl.BlockSpec(memory_space=pltpu.VMEM)
    smem = pl.BlockSpec(memory_space=pltpu.SMEM)
    steps = 3 * (units // 64 if units % 64 == 0 else 1)
    wide = jax.ShapeDtypeStruct(like.shape, BF16)
    return pl.pallas_call(
        finish_kernel,
        out_shape=(jax.ShapeDtypeStruct(grads.shape, BF16), wide, wide, wide),
        in_specs=[vmem] * 5 + [smem] * 2,
        out_specs=(hbm,) * 4,
        scratch_shapes=[
            pltpu.VMEM((3, units, features), BF16),
            pltpu.VMEM(grads.shape, BF16),
            pltpu.SemaphoreType.DMA((steps,)),
            pltpu.SemaphoreType.DMA,
        ],
        compiler_params=pltpu.CompilerParams(vmem_limit_bytes=32 << 20),
        name="finish",
    )(inputs, cotangents, backs, returned, grads, slots, weights)


def solution(mesh):
    def body(tokens, gate_weight, up_weight, down_weight, slot_tokens, slot_weights, out_grad):
        inputs, cotangents, backs, returned = exchange(
            mesh, tokens, gate_weight, up_weight, down_weight, slot_tokens, slot_weights, out_grad)
        return finish(
            inputs, cotangents, backs, returned, out_grad, slot_tokens, slot_weights, gate_weight)

    split = P("dp", "expert")
    wide = P("expert", "dp", None)
    slot = P(None, "dp")
    return jax.shard_map(
        body, mesh=mesh,
        in_specs=(split, wide, wide, wide, slot, slot, split),
        out_specs=(split, wide, wide, wide),
        check_vma=False)
```

```python
import functools

import jax
import jax.numpy as jnp
from jax import lax
from jax.experimental import pallas as pl
from jax.experimental.pallas import tpu as pltpu
from jax.sharding import PartitionSpec as P

MESH = pl.DeviceIdType.MESH
LANES = 128
F32 = jnp.float32
BF16 = jnp.bfloat16


def up_to(value, unit):
    return -(-value // unit) * unit


def each(count, body):
    if count <= 32:
        for i in range(count):
            body(i)
    else:
        lax.fori_loop(0, count, lambda i, carry: (body(i), carry)[1], 0)


def total_of(count, term, zero):
    if count <= 32:
        return sum((term(i) for i in range(1, count)), term(0))
    return lax.fori_loop(0, count, lambda i, value: value + term(i), zero)


def across(a, b):
    return lax.dot_general(a, b, (((1,), (1,)), ((), ())), preferred_element_type=F32)


def exchange_kernel(
    rows, experts, tokens, grads, gate_w, up_w, down_w, slots, weights,
    inputs_out, cotangents_out, backs_out, returned,
    tokens_v, grads_v, weights_v, stage, held, spread, sums, parts,
    load_sem, weight_sem, s1, r1, s2, r2,
):
    row, col = lax.axis_index("dp"), lax.axis_index("expert")
    width = tokens.shape[1]
    pieces = width // LANES
    pad16 = stage.shape[1]
    pad8 = returned.shape[1]

    loads = [
        pltpu.make_async_copy(source, target, load_sem.at[i])
        for i, (source, target) in enumerate((
            (tokens, tokens_v), (grads, grads_v)))
    ]
    weight_loads = [
        pltpu.make_async_copy(ref.at[0], weights_v.at[i], weight_sem.at[i])
        for i, ref in enumerate((gate_w, up_w, down_w))
    ]
    for load in loads:
        load.start()

    count = rows * experts
    me = row * experts + col

    def other(i):
        at = lax.rem(me + i + 1, count)
        return at, at // experts, lax.rem(at, experts)

    barrier = pltpu.get_barrier_semaphore()

    def greet(i):
        _, to_row, to_col = other(i)
        pl.semaphore_signal(barrier, inc=1, device_id=(to_row, to_col), device_id_type=MESH)

    each(count - 1, greet)
    for load in weight_loads:
        load.start()

    def column(line, kind, lanes):
        at = lax.broadcasted_iota(jnp.int32, (experts, lanes), 0)
        value = jnp.zeros((experts, lanes), kind)
        for e in range(experts):
            value = jnp.where(at == e, line[0, e], value)
        return value

    slot = column(slots, jnp.int32, tokens.shape[0])
    scale = column(weights, F32, width)
    hot = (
        lax.broadcasted_iota(jnp.int32, (experts, tokens.shape[0]), 1) == slot
    ).astype(F32).astype(BF16)
    loads[0].wait()
    picked = jnp.dot(hot, tokens_v[...], preferred_element_type=F32)
    loads[1].wait()
    scaled = scale * jnp.dot(hot, grads_v[...], preferred_element_type=F32)
    block = [picked[:, j * LANES:(j + 1) * LANES][:, None] for j in range(pieces)]
    block += [scaled[:, j * LANES:(j + 1) * LANES][:, None] for j in range(pieces)]
    if pad16 > 2 * pieces:
        block.append(jnp.zeros((experts, pad16 - 2 * pieces, LANES), F32))
    stage[...] = jnp.concatenate(block, axis=1).astype(BF16)
    mine = pl.ds(pl.multiple_of(col * pad16, pad16), pad16)
    held[row, mine] = stage[col]
    pl.semaphore_wait(barrier, count - 1)

    def direct(to, to_row, to_col, source, source_row, source_col):
        at = pl.ds(pl.multiple_of(source_col * pad16, pad16), pad16)
        return pltpu.make_async_remote_copy(
            src_ref=stage.at[to_col], dst_ref=held.at[source_row, at],
            send_sem=s1.at[to], recv_sem=r1.at[source],
            device_id=(to_row, to_col), device_id_type=MESH)

    each(count - 1, lambda i: direct(*other(i), me, row, col).start())

    def widen(source):
        size = experts * pad16
        spread[pl.ds(pl.multiple_of(source * size, size), size)] = held[source].astype(F32)

    each(count - 1, lambda i: direct(me, row, col, *other(i)).wait_recv())
    each(rows, widen)

    def whole_rows(base):
        return jnp.concatenate([
            spread[pl.ds(z * pad16 + base + j, rows, stride=experts * pad16), :]
            for z in range(experts) for j in range(pieces)
        ], axis=1).astype(BF16)

    inputs = whole_rows(0)
    cotangents = whole_rows(pieces)
    inputs_out[...] = inputs
    cotangents_out[...] = cotangents

    weight_loads[0].wait()
    gate_pre = across(inputs, weights_v[0])
    weight_loads[1].wait()
    up_pre = across(inputs, weights_v[1])
    weight_loads[2].wait()
    hidden_grad = across(cotangents, weights_v[2])
    sigmoid = jax.nn.sigmoid(gate_pre)
    activated = gate_pre * sigmoid
    hidden = (activated * up_pre).astype(BF16)
    gate_back = (
        hidden_grad * up_pre * sigmoid * (1.0 + gate_pre * (1.0 - sigmoid))
    ).astype(BF16)
    up_back = (hidden_grad * activated).astype(BF16)
    part = jnp.dot(gate_back, weights_v[0], preferred_element_type=F32)
    part += jnp.dot(up_back, weights_v[1], preferred_element_type=F32)
    for z in range(experts):
        for j in range(pieces):
            at = (z * pieces + j) * LANES
            parts[pl.ds(z * pad8 + j, rows, stride=experts * pad8), :] = part[:, at:at + LANES]

    def straight(to, to_row, to_col, source):
        at = pl.ds(pl.multiple_of(to * pad8, pad8), pad8)
        return pltpu.make_async_remote_copy(
            src_ref=parts.at[at], dst_ref=sums.at[source],
            send_sem=s2.at[to], recv_sem=r2.at[source],
            device_id=(to_row, to_col), device_id_type=MESH)

    each(count - 1, lambda i: straight(*other(i), me).start())
    for i, value in enumerate((gate_back, up_back, hidden)):
        backs_out[i] = value
    sums[me] = parts[pl.ds(pl.multiple_of(me * pad8, pad8), pad8)]
    each(count - 1, lambda i: straight(me, row, col, other(i)[0]).wait_recv())
    for e in range(experts):
        returned[e] = total_of(
            rows, lambda d, e=e: sums[d * experts + e], jnp.zeros((pad8, LANES), F32))

    each(count - 1, lambda i: direct(*other(i), me, row, col).wait_send())
    each(count - 1, lambda i: straight(*other(i), me).wait_send())


def exchange(mesh, tokens, gate_w, up_w, down_w, slots, weights, grads):
    rows, experts = mesh.shape["dp"], mesh.shape["expert"]
    width = tokens.shape[1]
    units, features = gate_w.shape[1:]
    pieces = width // LANES
    pad16, pad8 = up_to(2 * pieces, 16), up_to(pieces, 8)
    dma = pltpu.SemaphoreType.DMA
    hbm = pl.BlockSpec(memory_space=pltpu.HBM)
    vmem = pl.BlockSpec(memory_space=pltpu.VMEM)
    return pl.pallas_call(
        functools.partial(exchange_kernel, rows, experts),
        out_shape=(
            jax.ShapeDtypeStruct((rows, features), BF16),
            jax.ShapeDtypeStruct((rows, features), BF16),
            jax.ShapeDtypeStruct((3, rows, units), BF16),
            jax.ShapeDtypeStruct((experts, pad8, LANES), F32),
        ),
        in_specs=[hbm] * 5 + [pl.BlockSpec(memory_space=pltpu.SMEM)] * 2,
        out_specs=(vmem,) * 4,
        scratch_shapes=[
            pltpu.VMEM(tokens.shape, BF16),
            pltpu.VMEM(grads.shape, BF16),
            pltpu.VMEM((3, units, features), BF16),
            pltpu.VMEM((experts, pad16, LANES), BF16),
            pltpu.VMEM((rows, experts * pad16, LANES), BF16),
            pltpu.VMEM((rows * experts * pad16, LANES), F32),
            pltpu.VMEM((rows * experts, pad8, LANES), F32),
            pltpu.VMEM((rows * experts * pad8, LANES), F32),
            dma((2,)), dma((3,)),
            *[dma((rows * experts,))] * 4,
        ],
        compiler_params=pltpu.CompilerParams(
            collective_id=0, has_side_effects=True, vmem_limit_bytes=55000 << 10),
        name="exchange",
    )(tokens, grads, gate_w, up_w, down_w, slots, weights)


def finish_kernel(
    inputs, cotangents, backs, returned, grads, slots, weights,
    token_out, gate_out, up_out, down_out,
    wide, token_v, sems, token_sem,
):
    _, units, features = wide.shape
    experts = returned.shape[0]
    width = token_v.shape[1]
    chunk = 64 if units % 64 == 0 else units
    copies = []
    for i, out in enumerate((gate_out, up_out, down_out)):
        back = backs[i].astype(F32).T.astype(BF16)
        other = cotangents if i == 2 else inputs
        for k in range(units // chunk):
            at = pl.ds(k * chunk, chunk)
            wide[i, at] = jnp.dot(
                back[k * chunk:(k + 1) * chunk], other[...], preferred_element_type=F32
            ).astype(BF16)
            copy = pltpu.make_async_copy(
                wide.at[i, at], out.at[0, at], sems.at[i * (units // chunk) + k])
            copy.start()
            copies.append(copy)
    place = lax.broadcasted_iota(jnp.int32, (token_v.shape[0], LANES), 0)
    masks = [place == slots[0, e] for e in range(experts)]
    for j in range(width // LANES):
        at = pl.ds(j * LANES, LANES)
        value = grads[:, at].astype(F32)
        for e in range(experts):
            line = weights[0, e] * returned[e, pl.ds(j, 1), :]
            value += jnp.where(masks[e], line, 0.0)
        token_v[:, at] = value.astype(BF16)
    copy = pltpu.make_async_copy(token_v, token_out, token_sem)
    copy.start()
    copies.append(copy)
    for copy in copies:
        copy.wait()


def finish(inputs, cotangents, backs, returned, grads, slots, weights, like):
    units, features = like.shape[1:]
    hbm = pl.BlockSpec(memory_space=pl.ANY)
    vmem = pl.BlockSpec(memory_space=pltpu.VMEM)
    smem = pl.BlockSpec(memory_space=pltpu.SMEM)
    steps = 3 * (units // 64 if units % 64 == 0 else 1)
    wide = jax.ShapeDtypeStruct(like.shape, BF16)
    return pl.pallas_call(
        finish_kernel,
        out_shape=(jax.ShapeDtypeStruct(grads.shape, BF16), wide, wide, wide),
        in_specs=[vmem] * 5 + [smem] * 2,
        out_specs=(hbm,) * 4,
        scratch_shapes=[
            pltpu.VMEM((3, units, features), BF16),
            pltpu.VMEM(grads.shape, BF16),
            pltpu.SemaphoreType.DMA((steps,)),
            pltpu.SemaphoreType.DMA,
        ],
        compiler_params=pltpu.CompilerParams(vmem_limit_bytes=32 << 20),
        name="finish",
    )(inputs, cotangents, backs, returned, grads, slots, weights)


def solution(mesh):
    def body(tokens, gate_weight, up_weight, down_weight, slot_tokens, slot_weights, out_grad):
        slot_tokens, slot_weights = slot_tokens.reshape(1, -1), slot_weights.reshape(1, -1)
        inputs, cotangents, backs, returned = exchange(
            mesh, tokens, gate_weight, up_weight, down_weight, slot_tokens, slot_weights, out_grad)
        return finish(
            inputs, cotangents, backs, returned, out_grad, slot_tokens, slot_weights, gate_weight)

    split = P("dp", "expert")
    wide = P("expert", "dp", None)
    slot = P(None, "dp")
    return jax.shard_map(
        body, mesh=mesh,
        in_specs=(split, wide, wide, wide, slot, slot, split),
        out_specs=(split, wide, wide, wide),
        check_vma=False)
```
